512 devices in a mesh: tile: 16 (over y, x_lo), date: 32 (over z, x_hi, core).
Axes of the slice: x: 4 (x_hi: 2, x_lo: 2; x = x_hi * 2 + x_lo), y: 8, z: 8, core: 2. Of those that a mesh axis runs over, the one named last changes fastest.
Arguments:
- primary: bfloat16 [32, 16, 4096], P('tile', None, 'date'), parts along dimension 0, may hold values from -6 to 6
- secondaries: bfloat16 [64, 32, 32, 4224], P('date', 'tile'), parts along dimension 1, may hold values from -6 to 6
- shift_az: int32 [1024], P(('tile', 'date')), parts along dimension 0, may hold values from 0 to 8
- shift_rg: int32 [1024], P(('tile', 'date')), parts along dimension 0, may hold values from 0 to 120
- frac_index: int32 [64, 32], P('date', 'tile'), parts along dimension 1, may hold values from 0 to 63
Outputs:
- filtered: float32 [32, 64, 1024], P('tile', None, 'date'), parts along dimension 0
The draws below stay inside these ranges and needn't reach their ends.
There are 16 independent parts, one for each index of `tile`. The reference program is written for one: setup_inputs(seed, part) draws one part's arguments, and reference() takes and returns one part's arrays. A program takes and returns all parts, laid end to end along the dimension named above; each array names one. Nothing has to cross between parts.
All inputs are finite; a program needn't handle non-finite values.
Results may differ from the reference program's by a relative error of at most 0.0028.
Values may be sent and summed in bfloat16 or wider, within the bound.
A program may use at most 64 MiB of HBM per device.

```python
import jax
import jax.numpy as jnp
from jax import lax

DATES = 64
AZ = 16
RG = 4096
MARGIN_A = 16
MARGIN_R = 128
FRAC = 64
LOOK_AZ = 4
LOOK_RG = 16
ML_PIX = 1024


def place_ends(values, key, least, largest):
    dims = values.shape
    spot = [jax.random.randint(jax.random.fold_in(key, axis), (), 0, dims[axis]) for axis in range(len(dims))]
    values = values.at[tuple(spot)].set(least)
    longest = dims.index(max(dims))
    spot[longest] = (spot[longest] + 1) % dims[longest]
    return values.at[tuple(spot)].set(largest)


def shard_levels(stream_key, extent, cuts, smallest, high):
    factor_of = 1.0
    for position, blocks in cuts:
        heights = jax.random.uniform(jax.random.fold_in(jax.random.fold_in(stream_key, 6), position), (blocks,), jnp.float32, smallest / len(cuts), high / len(cuts))
        factor_of = factor_of * jnp.repeat(jnp.exp(heights), extent[position] // blocks).reshape((-1,) + (1,) * (len(extent) - 1 - position))
    return factor_of


def scatter_about(rng, extent, scale, reach, shards=(), kind=jnp.bfloat16):
    drawn = jax.random.normal(rng, extent, jnp.float32) * scale
    if len(shards) > 0:
        drawn = shard_levels(rng, extent, shards, -0.22, 0.18) * drawn
    return jnp.clip(drawn, min=-reach, max=reach).astype(kind)


def setup_inputs(seed: int = 0, part: int = 0) -> dict:
    splits = jax.random.split(jax.random.key(seed), 6)
    part_keys = jax.random.split(jax.random.fold_in(splits[5], part), 6)
    primary = scatter_about(part_keys[0], (2, AZ, RG), 1.0, 6.0, ((2, 32),))
    secondaries = scatter_about(part_keys[1], (DATES, 2, AZ + MARGIN_A, RG + MARGIN_R), 1.0, 6.0, ((0, 32),))
    shift_az = place_ends(jax.random.randint(part_keys[2], (DATES,), 0, MARGIN_A - 7), jax.random.fold_in(part_keys[2], 1), 0, (MARGIN_A - 7) - 1).astype(jnp.int32)
    shift_rg = place_ends(jax.random.randint(part_keys[3], (DATES,), 0, MARGIN_R - 7), jax.random.fold_in(part_keys[3], 1), 0, (MARGIN_R - 7) - 1).astype(jnp.int32)
    frac_index = place_ends(jax.random.randint(part_keys[4], (DATES, 2), 0, FRAC), jax.random.fold_in(part_keys[4], 1), 0, FRAC - 1).astype(jnp.int32)
    return {"primary": primary, "secondaries": secondaries, "shift_az": shift_az, "shift_rg": shift_rg, "frac_index": frac_index}


def sinc_taps(index):
    frac = index.astype(jnp.float32) / FRAC
    t = jnp.arange(8, dtype=jnp.float32) - 3.0 - frac
    return jnp.sinc(t) * (0.5 + 0.5 * jnp.cos(jnp.pi * t / 4.0))

def resample(slab, off_az, off_rg, fracs):
    taps_az = sinc_taps(fracs[0])
    taps_rg = sinc_taps(fracs[1])
    width = slab.shape[2]
    along = jnp.zeros((2, AZ, width), jnp.float32)
    for i in range(8):
        piece = lax.dynamic_slice(slab, (jnp.int32(0), (off_az + i).astype(jnp.int32), jnp.int32(0)), (2, AZ, width))
        along = along + taps_az[i] * piece.astype(jnp.float32)
    result = jnp.zeros((2, AZ, RG), jnp.float32)
    for j in range(8):
        piece = lax.dynamic_slice(along, (jnp.int32(0), jnp.int32(0), (off_rg + j).astype(jnp.int32)), (2, AZ, RG))
        result = result + taps_rg[j] * piece
    return result.astype(jnp.bfloat16)

def box_mean(values):
    lead = values.shape[:-2]
    lines, samples = values.shape[-2:]
    shaped = values.reshape(lead + (lines // LOOK_AZ, LOOK_AZ, samples // LOOK_RG, LOOK_RG))
    return shaped.mean(axis=(-3, -1))

def per_date(args):
    slab, off_az, off_rg, fracs, prim = args
    done = resample(slab, off_az, off_rg, fracs).astype(jnp.float32)
    sec_re, sec_im = (done[0], done[1])
    prim_re, prim_im = (prim[0], prim[1])
    ifg_re = sec_re * prim_re + sec_im * prim_im
    ifg_im = sec_im * prim_re - sec_re * prim_im
    return (box_mean(ifg_re), box_mean(ifg_im), box_mean(sec_re * sec_re + sec_im * sec_im))

def reference(primary, secondaries, shift_az, shift_rg, frac_index):
    prim = primary.astype(jnp.float32)

    def step(args):
        return per_date(args + (prim,))
    sum_re, sum_im, power_sec = lax.map(step, (secondaries, shift_az, shift_rg, frac_index))
    power_prim = box_mean(prim[0] * prim[0] + prim[1] * prim[1])
    scale = jnp.sqrt(float(LOOK_AZ * LOOK_RG)) / jnp.sqrt((power_prim[None] + 1e-06) * (power_sec + 1e-06))
    coh_re = jnp.transpose(sum_re * scale, (0, 2, 1)).reshape(DATES, ML_PIX)
    coh_im = jnp.transpose(sum_im * scale, (0, 2, 1)).reshape(DATES, ML_PIX)
    spread = DATES / 8.0
    order = jnp.arange(DATES, dtype=jnp.float32)
    weights = jnp.exp(-(order[:, None] - order[None, :]) ** 2 / (2.0 * spread * spread))
    weights = weights / lax.optimization_barrier(jnp.sum(weights, axis=1, keepdims=True))
    out_re = coh_re - jnp.dot(weights, coh_re, precision=lax.Precision.HIGHEST)
    out_im = coh_im - jnp.dot(weights, coh_im, precision=lax.Precision.HIGHEST)
    return jnp.stack([out_re, out_im])
```

```python
import functools

import jax
import jax.numpy as jnp
from jax import lax
from jax.experimental import pallas as pl
from jax.experimental.pallas import tpu as pltpu
from jax.sharding import PartitionSpec as P

F32 = jnp.float32
BF16 = jnp.bfloat16
AZ = 16
RG = 4096
WIDTH = 4224
BLOCK = 128
NB = RG // BLOCK
MESH = pl.DeviceIdType.MESH


def iota(shape, dim):
    return lax.broadcasted_iota(jnp.int32, shape, dim)


def split(x):
    hi = x.astype(BF16)
    return hi, (x - hi.astype(F32)).astype(BF16)


def dot(a, b):
    return jnp.dot(a, b, preferred_element_type=F32)


def taps_of(index):
    i = iota((8, 128), 0)
    t = i.astype(F32) - 3.0 - index.astype(F32) / 64.0
    pt = jnp.pi * t
    sinc = jnp.where(t == 0.0, 1.0, jnp.sin(pt) / jnp.where(t == 0.0, 1.0, pt))
    return sinc * (0.5 + 0.5 * jnp.cos(pt / 4.0))


def azimuth_matrix(a, taps):
    row, col = iota((64, 128), 0), iota((64, 128), 1)
    line = (row % 4) * 4 + (row // 8) % 4
    first = row < 32
    same = (row // 32 == col // 64) & ((row // 4) % 2 == (col // 32) % 2)
    u = col % 32 - line - jnp.where(first, a[0], a[1])
    out = jnp.zeros((64, 128), F32)
    for j in range(8):
        out = jnp.where(u == j, jnp.where(first, taps[0][j : j + 1], taps[1][j : j + 1]), out)
    return jnp.where(same, out, 0.0)


def range_matrix(r, taps):
    u = iota((256, 128), 0) - iota((256, 128), 1) - r
    out = jnp.zeros((256, 128), F32)
    for j in range(8):
        out = jnp.where(u == j, taps[j : j + 1], out)
    return out


def kernel(
    saz, srg, frac, prim_ref, sec_ref, out_ref,
    slab, along, perm, gath, msg, rx, slab_sem, psend, precv, msend, mrecv,
):
    n = NB
    me = lax.axis_index("date")
    chunks = 3
    cw = WIDTH // chunks

    def load(c):
        cols = pl.ds(c * cw, cw)
        return pltpu.make_async_copy(sec_ref.at[:, cols], slab.at[:, cols], slab_sem.at[c])

    for c in range(chunks):
        load(c).start()

    barrier = pltpu.get_barrier_semaphore()

    @pl.loop(1, n)
    def _(k):
        pl.semaphore_signal(barrier, inc=1, device_id={"date": lax.rem(me + k, n)}, device_id_type=MESH)

    row, col = iota((32, 32), 0), iota((32, 32), 1)
    want = ((row // 4) % 2) * 16 + (row % 4) * 4 + row // 8
    order = jnp.where(col == want, 1.0, 0.0).astype(BF16)
    mine = dot(order, prim_ref[...]).astype(BF16)
    perm[...] = mine
    gath[me] = mine

    pl.semaphore_wait(barrier, n - 1)

    def prim_copy(k, src, dst):
        return pltpu.make_async_remote_copy(
            src_ref=perm, dst_ref=gath.at[src], send_sem=psend.at[k], recv_sem=precv.at[src],
            device_id={"date": dst}, device_id_type=MESH,
        )

    @pl.loop(1, n)
    def _(k):
        prim_copy(k, me, lax.rem(me + k, n)).start()

    taps = [[taps_of(frac[d, x]) for x in range(2)] for d in range(2)]
    a_hi, a_lo = split(azimuth_matrix((saz[0], saz[1]), (taps[0][0], taps[1][0])))
    a_both = jnp.concatenate([a_hi, a_lo], axis=0)
    for c in range(chunks):
        load(c).wait()
        cols = pl.ds(c * cw, cw)
        y = dot(a_both, slab[:, cols])
        hi, lo = split(y[:64] + y[64:])
        for d in range(2):
            along[d, :32, cols] = hi[32 * d : 32 * d + 32]
            along[d, 32:, cols] = lo[32 * d : 32 * d + 32]

    res = []
    for d in range(2):
        b_hi, b_lo = split(range_matrix(srg[d], taps[d][1]))
        b_both = jnp.concatenate([b_hi, b_lo], axis=1)
        whole = along[d]
        rows = jnp.concatenate([whole[:, BLOCK * b : BLOCK * b + 256] for b in range(n)], axis=0)
        y = dot(rows, b_both).reshape(n, 64, 256)
        full = y[:, :32, :128] + (y[:, :32, 128:] + y[:, 32:, :128])
        res.append(full.astype(BF16).astype(F32).reshape(n, 4, 8, 128))

    @pl.loop(1, n)
    def _(k):
        src = lax.rem(me + n - k, n)
        prim_copy(k, src, src).wait_recv()

    p = gath[...].astype(F32).reshape(n, 4, 8, 128)
    swapped = jnp.concatenate([p[:, :, 4:], p[:, :, :4]], axis=2)
    kinds = []
    for d in range(2):
        kinds += [jnp.sum(res[d] * p, axis=1), jnp.sum(res[d] * swapped, axis=1)]
    kinds += [jnp.sum(res[d] * res[d], axis=1) for d in range(2)]
    kinds += [jnp.sum(p * p, axis=1)]
    x = jnp.stack(kinds, axis=1).reshape(n * 7 * 8, 128)
    x_hi, x_lo = split(x)
    x_both = jnp.concatenate([x_hi, x_lo], axis=1)
    look = (iota((256, 128), 0) % 128) // 16
    box = jnp.where(look == (iota((256, 128), 1) % 32) // 4, 1.0, 0.0).astype(BF16)
    y = dot(x_both, box).reshape(n, 7, 8, 128)
    sub, lane = iota((8, 128), 0), iota((8, 128), 1)
    hit = jnp.where(sub % 4 == lane % 4, 1.0 / 64.0, 0.0)
    flip = jnp.where(sub < 4, -hit, hit)
    of = lane // 32
    zero = jnp.zeros_like(hit)
    s = jnp.zeros((n, 8, 128), F32)
    for k in range(4):
        s = s + y[:, k] * jnp.where(of == k, flip if k % 2 else hit, zero)[None]
    q = y[:, 4] * jnp.where(of < 2, hit, zero)[None] + y[:, 5] * jnp.where(of < 2, zero, hit)[None]
    pw = y[:, 6] * hit[None]
    s, q, pw = jnp.sum(s, axis=1), jnp.sum(q, axis=1), jnp.sum(pw, axis=1)
    coherent = s * (8.0 / jnp.sqrt((pw + 1e-06) * (q + 1e-06)))
    msg[...] = coherent.reshape(n, 1, 128)
    rx[me] = msg[me]

    def msg_copy(k, src, dst):
        return pltpu.make_async_remote_copy(
            src_ref=msg.at[dst], dst_ref=rx.at[src], send_sem=msend.at[k], recv_sem=mrecv.at[src],
            device_id={"date": dst}, device_id_type=MESH,
        )

    @pl.loop(1, n)
    def _(k):
        msg_copy(k, me, lax.rem(me + k, n)).start()

    row, col = iota((64, 256), 0), iota((64, 256), 1)
    gap = (row - ((col % 32) * 2 + (col // 32) % 2)).astype(F32)
    w = jnp.exp(-(gap * gap) / 128.0)
    total = jnp.sum(jnp.where(col < 64, w, 0.0), axis=1, keepdims=True)
    high = jnp.where(gap == 0.0, 1.0, 0.0) - w / total
    h_hi, h_lo = split(high)
    filt = jnp.where((col // 64) % 2 == 0, h_hi.astype(F32), h_lo.astype(F32)).astype(BF16)

    @pl.loop(1, n)
    def _(k):
        src = lax.rem(me + n - k, n)
        msg_copy(k, src, src).wait_recv()

    c = rx[...].reshape(n, 128)
    c = jnp.concatenate([c, pltpu.roll(c, 64, 1)], axis=0)
    c_hi, c_lo = split(c)
    out = dot(filt, jnp.concatenate([c_hi, c_hi, c_lo, c_lo], axis=0)).T
    out_ref[0] = out[:32]
    out_ref[1] = out[32:64]

    @pl.loop(1, n)
    def _(k):
        dst = lax.rem(me + k, n)
        prim_copy(k, me, dst).wait_send()
        msg_copy(k, me, dst).wait_send()


def shards(primary, secondaries, shift_az, shift_rg, frac_index):
    n = NB
    vmem = pl.BlockSpec(memory_space=pltpu.VMEM)
    smem = pl.BlockSpec(memory_space=pltpu.SMEM)
    out = pl.pallas_call(
        kernel,
        out_shape=jax.ShapeDtypeStruct((2, 32, 64), F32),
        in_specs=[smem, smem, smem, vmem, pl.BlockSpec(memory_space=pltpu.HBM)],
        out_specs=vmem,
        scratch_shapes=[
            pltpu.VMEM((128, WIDTH), BF16),
            pltpu.VMEM((2, 64, WIDTH), BF16),
            pltpu.VMEM((32, 128), BF16),
            pltpu.VMEM((n, 32, 128), BF16),
            pltpu.VMEM((n, 1, 128), F32),
            pltpu.VMEM((n, 1, 128), F32),
            pltpu.SemaphoreType.DMA((3,)),
            pltpu.SemaphoreType.DMA((n,)),
            pltpu.SemaphoreType.DMA((n,)),
            pltpu.SemaphoreType.DMA((n,)),
            pltpu.SemaphoreType.DMA((n,)),
        ],
        compiler_params=pltpu.CompilerParams(
            collective_id=0, has_side_effects=True, vmem_limit_bytes=64 * 2**20
        ),
    )(shift_az, shift_rg, frac_index, primary.reshape(32, 128), secondaries.reshape(128, WIDTH))
    return jnp.transpose(out, (0, 2, 1))


def solution(mesh):
    in_specs = (
        P("tile", None, "date"),
        P("date", "tile", None, None),
        P(("tile", "date")),
        P(("tile", "date")),
        P("date", "tile"),
    )
    out_specs = P("tile", None, "date")
    return jax.shard_map(shards, mesh=mesh, in_specs=in_specs, out_specs=out_specs, check_vma=False)
```

```python
import jax
import jax.numpy as jnp
from jax import lax
from jax.experimental import pallas as pl
from jax.experimental.pallas import tpu as pltpu
from jax.sharding import PartitionSpec as P

F32 = jnp.float32
BF16 = jnp.bfloat16
WIDTH = 4224
BLOCK = 128
NB = 32
HALF = NB // 2
PIECES = (0, 9, 17, 25, 33)
MESH = pl.DeviceIdType.MESH


def iota(shape, dim):
    return lax.broadcasted_iota(jnp.int32, shape, dim)


def split(x):
    hi = x.astype(BF16)
    return hi, (x - hi.astype(F32)).astype(BF16)


def dot(a, b):
    return jnp.dot(a, b, preferred_element_type=F32)


def taps_of(index):
    i = iota((8, 128), 0)
    t = i.astype(F32) - 3.0 - index.astype(F32) / 64.0
    pt = jnp.pi * t
    sinc = jnp.where(t == 0.0, 1.0, jnp.sin(pt) / jnp.where(t == 0.0, 1.0, pt))
    return sinc * (0.5 + 0.5 * jnp.cos(pt / 4.0))


def azimuth_matrix(a, taps):
    row, col = iota((64, 128), 0), iota((64, 128), 1)
    line = (row % 4) * 4 + (row // 8) % 4
    first = row < 32
    same = (row // 32 == col // 64) & ((row // 4) % 2 == (col // 32) % 2)
    u = col % 32 - line - jnp.where(first, a[0], a[1])
    out = jnp.zeros((64, 128), F32)
    for j in range(8):
        out = jnp.where(u == j, jnp.where(first, taps[0][j : j + 1], taps[1][j : j + 1]), out)
    return jnp.where(same, out, 0.0)


def range_matrix(r, taps):
    u = iota((256, 128), 0) - iota((256, 128), 1) - r
    out = jnp.zeros((256, 128), F32)
    for j in range(8):
        out = jnp.where(u == j, taps[j : j + 1], out)
    return out


def kernel(
    saz_ref, srg_ref, frac_ref, prim_ref, sec_ref, out_ref,
    saz, srg, frac, prim, slab, along, tx, rx, in_sem, send_sem, recv_sem, late_sem, go_sem,
):
    n = NB
    me = lax.axis_index("date")
    early = me < HALF

    small = [
        pltpu.make_async_copy(src, dst, in_sem.at[k])
        for k, (src, dst) in enumerate(((saz_ref, saz), (srg_ref, srg), (frac_ref, frac), (prim_ref, prim)))
    ]

    def piece(c):
        return pl.ds(PIECES[c] * BLOCK, (PIECES[c + 1] - PIECES[c]) * BLOCK)

    def load(c):
        return pltpu.make_async_copy(sec_ref.at[:, piece(c)], slab.at[:, piece(c)], in_sem.at[4 + c])

    for copy in small:
        copy.start()
    for c in range(4):
        load(c).start()

    barrier = pltpu.get_barrier_semaphore()

    @pl.when(early)
    def _():
        @pl.loop(0, n)
        def _(k):
            @pl.when(k != me)
            def _():
                pl.semaphore_signal(barrier, inc=1, device_id={"date": k}, device_id_type=MESH)

    for copy in small[:3]:
        copy.wait()
    taps = [[taps_of(frac[d, x]) for x in range(2)] for d in range(2)]
    a_hi, a_lo = split(azimuth_matrix((saz[0], saz[1]), (taps[0][0], taps[1][0])))
    a_both = jnp.concatenate([a_hi, a_lo], axis=0)
    b_both = []
    for d in range(2):
        b_hi, b_lo = split(range_matrix(srg[d], taps[d][1]))
        b_both.append(jnp.concatenate([b_hi, b_lo], axis=1))

    def resample(c):
        load(c).wait()
        y = dot(a_both, slab[:, piece(c)])
        hi, lo = split(y[:64] + y[64:])
        for d in range(2):
            along[d, :32, piece(c)] = hi[32 * d : 32 * d + 32]
            along[d, 32:, piece(c)] = lo[32 * d : 32 * d + 32]
        first = 8 * c
        for d in range(2):
            whole = along[d, :, pl.ds(first * BLOCK, 9 * BLOCK)]
            rows = jnp.concatenate([whole[:, BLOCK * b : BLOCK * b + 256] for b in range(8)], axis=0)
            y = dot(rows, b_both[d]).reshape(8, 64, 256)
            full = y[:, :32, :128] + (y[:, :32, 128:] + y[:, 32:, :128])
            tx[pl.ds(first, 8), pl.ds(32 * d, 32)] = full.astype(BF16)

    def block_copy(src, dst):
        return pltpu.make_async_remote_copy(
            src_ref=tx.at[dst], dst_ref=rx.at[src], send_sem=send_sem.at[dst], recv_sem=recv_sem.at[src],
            device_id={"date": dst}, device_id_type=MESH,
        )

    def send(lo, hi):
        @pl.loop(lo, hi)
        def _(k):
            @pl.when(k != me)
            def _():
                block_copy(me, k).start()

    resample(0)

    @pl.when(early)
    def _():
        pl.semaphore_wait(barrier, HALF - 1)

    @pl.when(jnp.logical_not(early))
    def _():
        pl.semaphore_wait(barrier, HALF)

        @pl.loop(0, HALF)
        def _(k):
            pl.semaphore_signal(late_sem.at[me // 4 - 4], inc=1, device_id={"date": k}, device_id_type=MESH)

    send(0, 8)
    resample(1)
    send(8, 16)
    resample(2)
    resample(3)

    @pl.when(early)
    def _():
        @pl.loop(0, 4)
        def _(j):
            plane = (me // 4 + 1 + j) % 4
            pl.semaphore_wait(late_sem.at[plane], 4)
            send(HALF + 4 * plane, HALF + 4 * plane + 4)

        @pl.when((me < 4) | (me >= 12))
        def _():
            first = HALF + me % 4 + 8 * (1 - me // 12)
            pl.semaphore_signal(go_sem, inc=1, device_id={"date": first}, device_id_type=MESH)
            pl.semaphore_signal(go_sem, inc=1, device_id={"date": first + 4}, device_id_type=MESH)

    @pl.when(jnp.logical_not(early))
    def _():
        pl.semaphore_wait(go_sem, 1)
        send(HALF, n)

    rx[me] = tx[me]

    small[3].wait()
    row, col = iota((32, 32), 0), iota((32, 32), 1)
    want = ((row // 4) % 2) * 16 + (row % 4) * 4 + row // 8
    order = jnp.where(col == want, 1.0, 0.0).astype(BF16)
    p = dot(order, prim[...]).reshape(4, 8, 128)
    swapped = jnp.concatenate([p[:, 4:], p[:, :4]], axis=1)

    look = (iota((256, 128), 0) % 128) // 16
    box = jnp.where(look == (iota((256, 128), 1) % 32) // 4, 1.0, 0.0).astype(BF16)
    sub, lane = iota((8, 128), 0), iota((8, 128), 1)
    hit = jnp.where(sub % 4 == lane % 4, 1.0 / 64.0, 0.0)
    part = lane // 32
    masks = (
        jnp.where(part == 0, hit, 0.0),
        jnp.where(part == 1, jnp.where(sub < 4, -hit, hit), 0.0),
        jnp.where(part >= 2, hit, 0.0),
    )

    def boxes(x):
        hi, lo = split(x)
        return dot(jnp.concatenate([hi, lo], axis=1), box)

    power = jnp.sum(boxes(jnp.sum(p * p, axis=0)) * hit, axis=0, keepdims=True)

    row, col = iota((64, 256), 0), iota((64, 256), 1)
    gap = (row - col % 64).astype(F32)
    w = jnp.exp(-(gap * gap) / 128.0)
    total = jnp.sum(jnp.where(col < 64, w, 0.0), axis=1, keepdims=True)
    high = jnp.where(gap == 0.0, 1.0, 0.0) - w / total
    h_hi, h_lo = split(high)
    filt = jnp.where((col // 64) % 2 == 0, h_hi.astype(F32), h_lo.astype(F32)).astype(BF16)

    means = []
    for lo, hi in ((0, 16), (16, 24), (24, 32)):
        count = 2 * (hi - lo)

        @pl.loop(lo, hi)
        def _(k):
            @pl.when(k != me)
            def _():
                block_copy(k, k).wait_recv()

        s = rx[lo:hi].astype(F32).reshape(count, 4, 8, 128)
        kinds = [jnp.sum(s * p[None], axis=1), jnp.sum(s * swapped[None], axis=1), jnp.sum(s * s, axis=1)]
        y = boxes(jnp.stack(kinds, axis=1).reshape(count * 24, 128)).reshape(count, 3, 8, 128)
        z = y[:, 0] * masks[0][None] + y[:, 1] * masks[1][None] + y[:, 2] * masks[2][None]
        means.append(jnp.sum(z, axis=1))
    z = jnp.concatenate(means, axis=0)
    q = jnp.where(iota((64, 128), 1) < 64, pltpu.roll(z, 64, 1), 1.0)
    c = z * (8.0 / jnp.sqrt((power + 1e-06) * (q + 1e-06)))
    c_hi, c_lo = split(c)
    out = dot(filt, jnp.concatenate([c_hi, c_hi, c_lo, c_lo], axis=0)).T
    out_ref[0] = out[:32]
    out_ref[1] = out[32:64]

    @pl.loop(0, n)
    def _(k):
        @pl.when(k != me)
        def _():
            block_copy(me, k).wait_send()


def shards(primary, secondaries, shift_az, shift_rg, frac_index):
    n = NB
    hbm = pl.BlockSpec(memory_space=pl.ANY)
    out = pl.pallas_call(
        kernel,
        out_shape=jax.ShapeDtypeStruct((2, 32, 64), F32),
        in_specs=[hbm] * 5,
        out_specs=pl.BlockSpec(memory_space=pltpu.VMEM),
        scratch_shapes=[
            pltpu.SMEM((2,), jnp.int32),
            pltpu.SMEM((2,), jnp.int32),
            pltpu.SMEM((2, 2), jnp.int32),
            pltpu.VMEM((32, 128), BF16),
            pltpu.VMEM((128, WIDTH), BF16),
            pltpu.VMEM((2, 64, WIDTH), BF16),
            pltpu.VMEM((n, 64, 128), BF16),
            pltpu.VMEM((n, 64, 128), BF16),
            pltpu.SemaphoreType.DMA((8,)),
            pltpu.SemaphoreType.DMA((n,)),
            pltpu.SemaphoreType.DMA((n,)),
            pltpu.SemaphoreType.REGULAR((4,)),
            pltpu.SemaphoreType.REGULAR,
        ],
        compiler_params=pltpu.CompilerParams(
            collective_id=0, has_side_effects=True, vmem_limit_bytes=64 * 2**20
        ),
    )(shift_az, shift_rg, frac_index, primary.reshape(32, 128), secondaries.reshape(128, WIDTH))
    return jnp.transpose(out, (0, 2, 1))


def solution(mesh):
    in_specs = (
        P("tile", None, "date"),
        P("date", "tile", None, None),
        P(("tile", "date")),
        P(("tile", "date")),
        P("date", "tile"),
    )
    out_specs = P("tile", None, "date")
    return jax.shard_map(shards, mesh=mesh, in_specs=in_specs, out_specs=out_specs, check_vma=False)
```

```python
import jax
import jax.numpy as jnp
import numpy as np
from jax import lax
from jax.experimental import pallas as pl
from jax.experimental.pallas import tpu as pltpu
from jax.sharding import PartitionSpec as P

F32 = jnp.float32
BF16 = jnp.bfloat16
WIDTH = 4224
BLOCK = 128
NB = 32
HALF = NB // 2
PIECES = (0, 9, 17, 25, 33)
MESH = pl.DeviceIdType.MESH


def iota(shape, dim):
    return lax.broadcasted_iota(jnp.int32, shape, dim)


def split(x):
    hi = x.astype(BF16)
    return hi, (x - hi.astype(F32)).astype(BF16)


def dot(a, b):
    return jnp.dot(a, b, preferred_element_type=F32)


def tap_table():
    t = np.arange(8)[None] - 3.0 - np.arange(64)[:, None] / 64.0
    return (np.sinc(t) * (0.5 + 0.5 * np.cos(np.pi * t / 4.0))).astype(np.float32).reshape(-1)


def azimuth_matrix(a, taps):
    row, col = iota((32, 128), 0), iota((32, 128), 1)
    line = (row % 4) * 4 + row // 8
    same = (row // 4) % 2 == (col // 32) % 2
    dates = []
    for d in range(2):
        u = col % 32 - line - a[d]
        u = jnp.where(same & (col // 64 == d), u, -1)
        out = jnp.zeros((32, 128), F32)
        for j in range(8):
            out = jnp.where(u == j, taps[d][j], out)
        dates.append(out)
    return jnp.concatenate(dates, axis=0)


def range_matrix(r, taps):
    u = (iota((8, 128), 0) - iota((8, 128), 1) - r + 256) % 128
    rows = jnp.zeros((8, 128), F32)
    for j in range(8):
        rows = jnp.where(u == j, taps[j], rows)
    turned = [rows] + [pltpu.roll(rows, 8 * k, 1) for k in range(1, 16)]
    u = iota((256, 128), 0) - iota((256, 128), 1) - r
    return jnp.where((u >= 0) & (u < 8), jnp.concatenate(turned * 2, axis=0), 0.0)


def kernel(
    saz_ref, srg_ref, frac_ref, table_ref, prim_ref, sec_ref, out_ref,
    saz, srg, frac, table, prim, slab, along, tx, rx, in_sem, send_sem, recv_sem, late_sem, go_sem, turn_sem,
):
    n = NB
    me = lax.axis_index("date")
    early = me < HALF

    small = [
        pltpu.make_async_copy(src, dst, in_sem.at[k])
        for k, (src, dst) in enumerate(((saz_ref, saz), (srg_ref, srg), (frac_ref, frac), (table_ref, table), (prim_ref, prim)))
    ]

    def piece(c):
        return pl.ds(PIECES[c] * BLOCK, (PIECES[c + 1] - PIECES[c]) * BLOCK)

    def load(c):
        return pltpu.make_async_copy(sec_ref.at[:, piece(c)], slab.at[:, piece(c)], in_sem.at[5 + c])

    barrier = pltpu.get_barrier_semaphore()

    @pl.when(early)
    def _():
        for k in range(n - 1, HALF - 1, -1):
            pl.semaphore_signal(barrier, inc=1, device_id={"date": k}, device_id_type=MESH)

        @pl.loop(0, HALF)
        def _(k):
            @pl.when(k != me)
            def _():
                pl.semaphore_signal(barrier, inc=1, device_id={"date": k}, device_id_type=MESH)

    for copy in small:
        copy.start()
    for c in range(4):
        load(c).start()

    for copy in small[:4]:
        copy.wait()
    taps = [[[table[frac[d, x] * 8 + j] for j in range(8)] for x in range(2)] for d in range(2)]
    a_hi, a_lo = split(azimuth_matrix((saz[0], saz[1]), (taps[0][0], taps[1][0])))
    a_both = jnp.concatenate([a_hi, a_lo], axis=0)
    b_both = []
    for d in range(2):
        b_hi, b_lo = split(range_matrix(srg[d], taps[d][1]))
        b_both.append(jnp.concatenate([b_hi, b_lo], axis=1))

    def resample(c):
        load(c).wait()
        y = dot(a_both, slab[:, piece(c)])
        hi, lo = split(y[:64] + y[64:])
        for d in range(2):
            along[d, :32, piece(c)] = hi[32 * d : 32 * d + 32]
            along[d, 32:, piece(c)] = lo[32 * d : 32 * d + 32]
        first = 8 * c
        for d in range(2):
            whole = along[d, :, pl.ds(first * BLOCK, 9 * BLOCK)]
            rows = jnp.concatenate([whole[:, BLOCK * b : BLOCK * b + 256] for b in range(8)], axis=0)
            y = dot(rows, b_both[d]).reshape(8, 64, 256)
            full = y[:, :32, :128] + (y[:, :32, 128:] + y[:, 32:, :128])
            tx[pl.ds(first, 8), pl.ds(32 * d, 32)] = full.astype(BF16)

    def block_copy(src, dst):
        return pltpu.make_async_remote_copy(
            src_ref=tx.at[dst], dst_ref=rx.at[src], send_sem=send_sem.at[dst], recv_sem=recv_sem.at[src],
            device_id={"date": dst}, device_id_type=MESH,
        )

    def send(lo, hi):
        @pl.loop(lo, hi)
        def _(k):
            @pl.when(k != me)
            def _():
                block_copy(me, k).start()

    def sent(lo, hi):
        @pl.loop(lo, hi)
        def _(k):
            @pl.when(k != me)
            def _():
                block_copy(me, k).wait_send()

    plane = me // 4
    late = jnp.logical_not(early)

    @pl.when(early)
    def _():
        pl.semaphore_wait(barrier, HALF - 1)

    @pl.when(late)
    def _():
        pl.semaphore_wait(barrier, HALF)
        for k in range(HALF):
            pl.semaphore_signal(late_sem.at[plane - 4], inc=1, device_id={"date": k}, device_id_type=MESH)

    resample(0)
    send(0, 8)
    resample(1)

    send(8, 16)

    resample(2)
    resample(3)
    rx[me] = tx[me]

    small[4].wait()
    row, col = iota((32, 32), 0), iota((32, 32), 1)
    want = ((row // 4) % 2) * 16 + (row % 4) * 4 + row // 8
    order = jnp.where(col == want, 1.0, 0.0).astype(BF16)
    p = dot(order, prim[...]).reshape(4, 8, 128)
    swapped = jnp.concatenate([p[:, 4:], p[:, :4]], axis=1)

    look = (iota((256, 128), 0) % 128) // 16
    box = jnp.where(look == (iota((256, 128), 1) % 32) // 4, 1.0, 0.0).astype(BF16)
    sub, lane = iota((8, 128), 0), iota((8, 128), 1)
    hit = jnp.where(sub % 4 == lane % 4, 1.0 / 64.0, 0.0)
    part = lane // 32
    masks = (
        jnp.where(part == 0, hit, 0.0),
        jnp.where(part == 1, jnp.where(sub < 4, -hit, hit), 0.0),
        jnp.where(part >= 2, hit, 0.0),
    )

    def boxes(x):
        hi, lo = split(x)
        return dot(jnp.concatenate([hi, lo], axis=1), box)

    power = jnp.sum(boxes(jnp.sum(p * p, axis=0)) * hit, axis=0, keepdims=True)

    row, col = iota((64, 256), 0), iota((64, 256), 1)
    gap = (row - col % 64).astype(F32)
    w = jnp.exp(-(gap * gap) / 128.0)
    total = jnp.sum(jnp.where(col < 64, w, 0.0), axis=1, keepdims=True)
    high = jnp.where(gap == 0.0, 1.0, 0.0) - w / total
    h_hi, h_lo = split(high)
    filt = jnp.where((col // 64) % 2 == 0, h_hi.astype(F32), h_lo.astype(F32)).astype(BF16)

    @pl.when(late)
    def _():
        pl.semaphore_wait(go_sem, 1)
        send(HALF, n)

    @pl.when(early)
    def _():
        @pl.loop(0, 4)
        def _(to):
            pl.semaphore_wait(late_sem.at[to], 4)

            @pl.when((plane == 0) | ((plane == 1) & (to < 2)) | ((plane == 2) & (to < 2)) | ((plane == 3) & (to < 3)))
            def _():
                send(HALF + 4 * to, HALF + 4 * to + 4)

    @pl.when((plane == 0) | (plane == 3))
    def _():
        first = HALF + me % 4 + 8 * (1 - plane // 3)
        pl.semaphore_signal(go_sem, inc=1, device_id={"date": first}, device_id_type=MESH)
        pl.semaphore_signal(go_sem, inc=1, device_id={"date": first + 4}, device_id_type=MESH)

    def turn():
        @pl.when(plane == 0)
        def _():
            sent(16, 20)

            @pl.loop(1, 4)
            def _(k):
                pl.semaphore_signal(turn_sem, inc=1, device_id={"date": me + 4 * k}, device_id_type=MESH)

        @pl.when(early & (plane > 0))
        def _():
            pl.semaphore_wait(turn_sem, 1)

        @pl.when(plane == 1)
        def _():
            send(24, n)

        @pl.when(plane == 2)
        def _():
            send(24, n)

        @pl.when(plane == 3)
        def _():
            send(28, n)

    means = []
    for lo, hi in ((0, 16), (16, 24), (24, 32)):
        count = 2 * (hi - lo)

        @pl.loop(lo, hi)
        def _(k):
            @pl.when(k != me)
            def _():
                block_copy(k, k).wait_recv()

        s = rx[lo:hi].astype(F32).reshape(count, 4, 8, 128)
        kinds = [jnp.sum(s * p[None], axis=1), jnp.sum(s * swapped[None], axis=1), jnp.sum(s * s, axis=1)]
        y = boxes(jnp.stack(kinds, axis=1).reshape(count * 24, 128)).reshape(count, 3, 8, 128)
        z = y[:, 0] * masks[0][None] + y[:, 1] * masks[1][None] + y[:, 2] * masks[2][None]
        means.append(jnp.sum(z, axis=1))
        if lo == 0:
            turn()
    z = jnp.concatenate(means, axis=0)
    q = jnp.where(iota((64, 128), 1) < 64, pltpu.roll(z, 64, 1), 1.0)
    c = z * (8.0 / jnp.sqrt((power + 1e-06) * (q + 1e-06)))
    c_hi, c_lo = split(c)
    out = dot(filt, jnp.concatenate([c_hi, c_hi, c_lo, c_lo], axis=0)).T
    out_ref[0] = out[:32]
    out_ref[1] = out[32:64]

    sent(20, n)

    @pl.when(plane != 0)
    def _():
        sent(16, 20)

    sent(8, 16)

    sent(0, 8)


def shards(primary, secondaries, shift_az, shift_rg, frac_index):
    n = NB
    hbm = pl.BlockSpec(memory_space=pl.ANY)
    operands = (
        shift_az, shift_rg, frac_index, jnp.asarray(tap_table()), primary.reshape(32, 128), secondaries.reshape(128, WIDTH),
    )
    operands = [pltpu.with_memory_space_constraint(x, pltpu.HBM) for x in operands]
    out = pl.pallas_call(
        kernel,
        out_shape=pltpu.VMEM((2, 32, 64), F32),
        in_specs=[hbm] * 6,
        out_specs=pl.BlockSpec(memory_space=pltpu.VMEM),
        scratch_shapes=[
            pltpu.SMEM((2,), jnp.int32),
            pltpu.SMEM((2,), jnp.int32),
            pltpu.SMEM((2, 2), jnp.int32),
            pltpu.SMEM((512,), F32),
            pltpu.VMEM((32, 128), BF16),
            pltpu.VMEM((128, WIDTH), BF16),
            pltpu.VMEM((2, 64, WIDTH), BF16),
            pltpu.VMEM((n, 64, 128), BF16),
            pltpu.VMEM((n, 64, 128), BF16),
            pltpu.SemaphoreType.DMA((9,)),
            pltpu.SemaphoreType.DMA((n,)),
            pltpu.SemaphoreType.DMA((n,)),
            pltpu.SemaphoreType.REGULAR((4,)),
            pltpu.SemaphoreType.REGULAR,
            pltpu.SemaphoreType.REGULAR,
        ],
        compiler_params=pltpu.CompilerParams(
            collective_id=0, has_side_effects=True, vmem_limit_bytes=48 * 2**20
        ),
    )(*operands)
    return jnp.transpose(out, (0, 2, 1))


def solution(mesh):
    in_specs = (
        P("tile", None, "date"),
        P("date", "tile", None, None),
        P(("tile", "date")),
        P(("tile", "date")),
        P("date", "tile"),
    )
    out_specs = P("tile", None, "date")
    return jax.shard_map(shards, mesh=mesh, in_specs=in_specs, out_specs=out_specs, check_vma=False)
```

```python
import jax
import jax.numpy as jnp
import numpy as np
from jax import lax
from jax.experimental import pallas as pl
from jax.experimental.pallas import tpu as pltpu
from jax.sharding import PartitionSpec as P

F32 = jnp.float32
BF16 = jnp.bfloat16
WIDTH = 4224
BLOCK = 128
NB = 32
PLANES = 4
FIRST_LATE = 4 * PLANES
PIECES = (0, 5, 9, 17, 25, 33)
FIRST = (0, 4, 8, 16, 24, 32)
MESH = pl.DeviceIdType.MESH


def iota(shape, dim):
    return lax.broadcasted_iota(jnp.int32, shape, dim)


def split(x):
    hi = x.astype(BF16)
    return hi, (x - hi.astype(F32)).astype(BF16)


def dot(a, b):
    return jnp.dot(a, b, preferred_element_type=F32)


def tap_table():
    t = np.arange(8)[None] - 3.0 - np.arange(64)[:, None] / 64.0
    return (np.sinc(t) * (0.5 + 0.5 * np.cos(np.pi * t / 4.0))).astype(np.float32).reshape(-1)


def azimuth_matrix(a, taps):
    row, col = iota((32, 128), 0), iota((32, 128), 1)
    line = (row % 4) * 4 + row // 8
    same = (row // 4) % 2 == (col // 32) % 2
    dates = []
    for d in range(2):
        u = col % 32 - line - a[d]
        u = jnp.where(same & (col // 64 == d), u, -1)
        out = jnp.zeros((32, 128), F32)
        for j in range(8):
            out = jnp.where(u == j, taps[d][j], out)
        dates.append(out)
    return jnp.concatenate(dates, axis=0)


def range_matrix(r, taps):
    u = (iota((8, 128), 0) - iota((8, 128), 1) - r + 256) % 128
    rows = jnp.zeros((8, 128), F32)
    for j in range(8):
        rows = jnp.where(u == j, taps[j], rows)
    turned = [rows] + [pltpu.roll(rows, 8 * k, 1) for k in range(1, 16)]
    u = iota((256, 128), 0) - iota((256, 128), 1) - r
    return jnp.where((u >= 0) & (u < 8), jnp.concatenate(turned * 2, axis=0), 0.0)


def kernel(
    saz_ref, srg_ref, frac_ref, table_ref, prim_ref, sec_ref, out_ref,
    saz, srg, frac, table, prim, slab, along, tx, rx, z_ref, in_sem, send_sem, recv_sem, late_sem, go_sem, turn_sem,
):
    n = NB
    me = lax.axis_index("date")
    plane = me // 4
    early = me < FIRST_LATE

    small = [
        pltpu.make_async_copy(src, dst, in_sem.at[k])
        for k, (src, dst) in enumerate(((saz_ref, saz), (srg_ref, srg), (frac_ref, frac), (table_ref, table), (prim_ref, prim)))
    ]

    def piece(c):
        return pl.ds(PIECES[c] * BLOCK, (PIECES[c + 1] - PIECES[c]) * BLOCK)

    def load(c):
        return pltpu.make_async_copy(sec_ref.at[:, piece(c)], slab.at[:, piece(c)], in_sem.at[5 + c])

    barrier = pltpu.get_barrier_semaphore()

    @pl.when(early)
    def _():
        for k in range(n - 1, FIRST_LATE - 1, -1):
            pl.semaphore_signal(barrier, inc=1, device_id={"date": k}, device_id_type=MESH)

        @pl.loop(0, FIRST_LATE)
        def _(k):
            @pl.when(k != me)
            def _():
                pl.semaphore_signal(barrier, inc=1, device_id={"date": k}, device_id_type=MESH)

    for copy in small:
        copy.start()
    for c in range(5):
        load(c).start()

    for copy in small[:4]:
        copy.wait()
    taps = [[[table[frac[d, x] * 8 + j] for j in range(8)] for x in range(2)] for d in range(2)]
    a_hi, a_lo = split(azimuth_matrix((saz[0], saz[1]), (taps[0][0], taps[1][0])))
    a_both = jnp.concatenate([a_hi, a_lo], axis=0)
    b_both = []
    for d in range(2):
        b_hi, b_lo = split(range_matrix(srg[d], taps[d][1]))
        b_both.append(jnp.concatenate([b_hi, b_lo], axis=1))

    def resample(c):
        load(c).wait()
        y = dot(a_both, slab[:, piece(c)])
        hi, lo = split(y[:64] + y[64:])
        for d in range(2):
            along[d, :32, piece(c)] = hi[32 * d : 32 * d + 32]
            along[d, 32:, piece(c)] = lo[32 * d : 32 * d + 32]
        first, many = FIRST[c], FIRST[c + 1] - FIRST[c]
        for d in range(2):
            whole = along[d, :, pl.ds(first * BLOCK, (many + 1) * BLOCK)]
            rows = jnp.concatenate([whole[:, BLOCK * b : BLOCK * b + 256] for b in range(many)], axis=0)
            y = dot(rows, b_both[d]).reshape(many, 64, 256)
            full = y[:, :32, :128] + (y[:, :32, 128:] + y[:, 32:, :128])
            tx[pl.ds(first, many), pl.ds(32 * d, 32)] = full.astype(BF16)

    def class_of(k):
        return ((k + n - FIRST_LATE) // n) * (k // 4 - PLANES + 1)

    def block_copy(src, dst):
        return pltpu.make_async_remote_copy(
            src_ref=tx.at[dst], dst_ref=rx.at[src],
            send_sem=send_sem.at[class_of(dst)], recv_sem=recv_sem.at[class_of(src)],
            device_id={"date": dst}, device_id_type=MESH,
        )

    def wait_class(c, full, mine, received):
        for count, here in ((full - 1, mine), (full, jnp.logical_not(mine))):

            @pl.when(here)
            def _():
                copy = pltpu.make_async_remote_copy(
                    src_ref=tx.at[pl.ds(0, count)], dst_ref=rx.at[pl.ds(0, count)],
                    send_sem=send_sem.at[c], recv_sem=recv_sem.at[c],
                    device_id={"date": (me + 1) % n}, device_id_type=MESH,
                )
                copy.wait_recv() if received else copy.wait_send()

    def send(lo, hi):
        @pl.loop(lo, hi)
        def _(k):
            @pl.when(k != me)
            def _():
                block_copy(me, k).start()

    late = jnp.logical_not(early)

    @pl.when(early)
    def _():
        pl.semaphore_wait(barrier, FIRST_LATE - 1)

    @pl.when(late)
    def _():
        pl.semaphore_wait(barrier, FIRST_LATE)
        for k in range(FIRST_LATE):
            pl.semaphore_signal(late_sem.at[plane - PLANES], inc=1, device_id={"date": k}, device_id_type=MESH)

    resample(0)
    send(0, 4)
    resample(1)
    send(4, 8)
    resample(2)
    send(8, FIRST_LATE)
    resample(3)
    resample(4)
    rx[me] = tx[me]

    small[4].wait()
    row, col = iota((32, 32), 0), iota((32, 32), 1)
    want = ((row // 4) % 2) * 16 + (row % 4) * 4 + row // 8
    order = jnp.where(col == want, 1.0, 0.0).astype(BF16)
    p = dot(order, prim[...]).reshape(4, 8, 128)
    swapped = jnp.concatenate([p[:, 4:], p[:, :4]], axis=1)

    look = (iota((256, 128), 0) % 128) // 16
    box = jnp.where(look == (iota((256, 128), 1) % 32) // 4, 1.0, 0.0).astype(BF16)
    sub, lane = iota((8, 128), 0), iota((8, 128), 1)
    hit = jnp.where(sub % 4 == lane % 4, 1.0 / 64.0, 0.0)
    part = lane // 32
    masks = (
        jnp.where(part == 0, hit, 0.0),
        jnp.where(part == 1, jnp.where(sub < 4, -hit, hit), 0.0),
        jnp.where(part >= 2, hit, 0.0),
    )

    def boxes(x):
        hi, lo = split(x)
        return dot(jnp.concatenate([hi, lo], axis=1), box)

    power = jnp.sum(boxes(jnp.sum(p * p, axis=0)) * hit, axis=0, keepdims=True)

    row, col = iota((64, 256), 0), iota((64, 256), 1)
    gap = (row - col % 64).astype(F32)
    w = jnp.exp(-(gap * gap) / 128.0)
    total = jnp.sum(jnp.where(col < 64, w, 0.0), axis=1, keepdims=True)
    high = jnp.where(gap == 0.0, 1.0, 0.0) - w / total
    h_hi, h_lo = split(high)
    filt = jnp.where((col // 64) % 2 == 0, h_hi.astype(F32), h_lo.astype(F32)).astype(BF16)

    @pl.when(late)
    def _():
        pl.semaphore_wait(go_sem, 1)
        send(FIRST_LATE, n)

    def held(to):
        return ((plane == 1) & (to >= 6)) | ((plane == 2) & (to >= 6)) | ((plane == 3) & (to >= 7))

    @pl.when(early)
    def _():
        @pl.loop(PLANES, 8)
        def _(to):
            pl.semaphore_wait(late_sem.at[to - PLANES], 4)

            @pl.when(jnp.logical_not(held(to)))
            def _():
                send(4 * to, 4 * to + 4)

    @pl.when(plane == 0)
    def _():
        for to in (6, 7):
            pl.semaphore_signal(go_sem, inc=1, device_id={"date": me % 4 + 4 * to}, device_id_type=MESH)

    @pl.when(plane == 3)
    def _():
        for to in (4, 5):
            pl.semaphore_signal(go_sem, inc=1, device_id={"date": me % 4 + 4 * to}, device_id_type=MESH)

    def turn():
        @pl.when(plane == 0)
        def _():
            wait_class(1, 4, plane == 4, False)

            @pl.loop(1, PLANES)
            def _(k):
                pl.semaphore_signal(turn_sem, inc=1, device_id={"date": me + 4 * k}, device_id_type=MESH)

        @pl.when(early & (plane > 0))
        def _():
            pl.semaphore_wait(turn_sem, 1)

            @pl.loop(PLANES, 8)
            def _(to):
                @pl.when(held(to))
                def _():
                    send(4 * to, 4 * to + 4)

    def process(rows):
        count = 2 * rows.shape[0]
        s = rows.astype(F32).reshape(count, 4, 8, 128)
        kinds = [jnp.sum(s * p[None], axis=1), jnp.sum(s * swapped[None], axis=1), jnp.sum(s * s, axis=1)]
        y = boxes(jnp.stack(kinds, axis=1).reshape(count * 24, 128)).reshape(count, 3, 8, 128)
        z = y[:, 0] * masks[0][None] + y[:, 1] * masks[1][None] + y[:, 2] * masks[2][None]
        return jnp.sum(z, axis=1)

    wait_class(0, FIRST_LATE, early, False)
    wait_class(0, FIRST_LATE, early, True)
    z_ref[pl.ds(0, 2 * FIRST_LATE)] = process(rx[:FIRST_LATE])
    turn()
    wait_class(1, 4, plane == 4, True)
    wait_class(2, 4, plane == 5, True)
    z_ref[pl.ds(32, 16)] = process(rx[16:24])
    wait_class(3, 4, plane == 6, True)
    wait_class(4, 4, plane == 7, True)
    z_ref[pl.ds(48, 16)] = process(rx[24:32])

    z = z_ref[...]
    q = jnp.where(iota((64, 128), 1) < 64, pltpu.roll(z, 64, 1), 1.0)
    c = z * (8.0 / jnp.sqrt((power + 1e-06) * (q + 1e-06)))
    c_hi, c_lo = split(c)
    out = dot(filt, jnp.concatenate([c_hi, c_hi, c_lo, c_lo], axis=0)).T
    out_ref[0] = out[:32]
    out_ref[1] = out[32:64]

    for to in range(PLANES, 8):
        if to != 4:
            wait_class(to - PLANES + 1, 4, plane == to, False)

    @pl.when(plane != 0)
    def _():
        wait_class(1, 4, plane == 4, False)


def shards(primary, secondaries, shift_az, shift_rg, frac_index):
    n = NB
    hbm = pl.BlockSpec(memory_space=pl.ANY)
    operands = (
        shift_az, shift_rg, frac_index, jnp.asarray(tap_table()), primary.reshape(32, 128), secondaries.reshape(128, WIDTH),
    )
    operands = [pltpu.with_memory_space_constraint(x, pltpu.HBM) for x in operands]
    out = pl.pallas_call(
        kernel,
        out_shape=pltpu.VMEM((2, 32, 64), F32),
        in_specs=[hbm] * 6,
        out_specs=pl.BlockSpec(memory_space=pltpu.VMEM),
        scratch_shapes=[
            pltpu.SMEM((2,), jnp.int32),
            pltpu.SMEM((2,), jnp.int32),
            pltpu.SMEM((2, 2), jnp.int32),
            pltpu.SMEM((512,), F32),
            pltpu.VMEM((32, 128), BF16),
            pltpu.VMEM((128, WIDTH), BF16),
            pltpu.VMEM((2, 64, WIDTH), BF16),
            pltpu.VMEM((n, 64, 128), BF16),
            pltpu.VMEM((n, 64, 128), BF16),
            pltpu.VMEM((64, 128), F32),
            pltpu.SemaphoreType.DMA((10,)),
            pltpu.SemaphoreType.DMA((9 - PLANES,)),
            pltpu.SemaphoreType.DMA((9 - PLANES,)),
            pltpu.SemaphoreType.REGULAR((8 - PLANES,)),
            pltpu.SemaphoreType.REGULAR,
            pltpu.SemaphoreType.REGULAR,
        ],
        compiler_params=pltpu.CompilerParams(
            collective_id=0, has_side_effects=True, vmem_limit_bytes=48 * 2**20
        ),
    )(*operands)
    return jnp.transpose(out, (0, 2, 1))


def solution(mesh):
    in_specs = (
        P("tile", None, "date"),
        P("date", "tile", None, None),
        P(("tile", "date")),
        P(("tile", "date")),
        P("date", "tile"),
    )
    out_specs = P("tile", None, "date")
    return jax.shard_map(shards, mesh=mesh, in_specs=in_specs, out_specs=out_specs, check_vma=False)
```

```python
import jax
import jax.numpy as jnp
import numpy as np
from jax import lax
from jax.experimental import pallas as pl
from jax.experimental.pallas import tpu as pltpu
from jax.sharding import PartitionSpec as P

F32 = jnp.float32
BF16 = jnp.bfloat16
WIDTH = 4224
BLOCK = 128
NB = 32
PLANES = 4
FIRST_LATE = 4 * PLANES
PIECES = (0, 5, 9, 17, 25, 33)
FIRST = (0, 4, 8, 16, 24, 32)
MESH = pl.DeviceIdType.MESH


def iota(shape, dim):
    return lax.broadcasted_iota(jnp.int32, shape, dim)


def split(x):
    hi = x.astype(BF16)
    return hi, (x - hi.astype(F32)).astype(BF16)


def dot(a, b):
    return jnp.dot(a, b, preferred_element_type=F32)


def tap_table():
    t = np.arange(8)[None] - 3.0 - np.arange(64)[:, None] / 64.0
    return (np.sinc(t) * (0.5 + 0.5 * np.cos(np.pi * t / 4.0))).astype(np.float32).reshape(-1)


def azimuth_matrix(a, taps):
    row, col = iota((32, 128), 0), iota((32, 128), 1)
    line = (row % 4) * 4 + row // 8
    same = (row // 4) % 2 == (col // 32) % 2
    dates = []
    for d in range(2):
        u = col % 32 - line - a[d]
        u = jnp.where(same & (col // 64 == d), u, -1)
        out = jnp.zeros((32, 128), F32)
        for j in range(8):
            out = jnp.where(u == j, taps[d][j], out)
        dates.append(out)
    return jnp.concatenate(dates, axis=0)


def range_matrix(r, taps):
    u = (iota((8, 128), 0) - iota((8, 128), 1) - r + 256) % 128
    rows = jnp.zeros((8, 128), F32)
    for j in range(8):
        rows = jnp.where(u == j, taps[j], rows)
    turned = [rows] + [pltpu.roll(rows, 8 * k, 1) for k in range(1, 16)]
    u = iota((256, 128), 0) - iota((256, 128), 1) - r
    return jnp.where((u >= 0) & (u < 8), jnp.concatenate(turned * 2, axis=0), 0.0)


def kernel(
    saz_ref, srg_ref, frac_ref, table_ref, prim_ref, sec_ref, out_ref,
    saz, srg, frac, table, prim, slab, along, tx, rx, z_ref, in_sem, send_sem, recv_sem, late_sem, go_sem, turn_sem,
):
    n = NB
    me = lax.axis_index("date")
    plane = me // 4
    early = me < FIRST_LATE

    small = [
        pltpu.make_async_copy(src, dst, in_sem.at[k])
        for k, (src, dst) in enumerate(((saz_ref, saz), (srg_ref, srg), (frac_ref, frac), (table_ref, table), (prim_ref, prim)))
    ]

    def piece(c):
        return pl.ds(PIECES[c] * BLOCK, (PIECES[c + 1] - PIECES[c]) * BLOCK)

    def load(c):
        return pltpu.make_async_copy(sec_ref.at[:, piece(c)], slab.at[:, piece(c)], in_sem.at[5 + c])

    barrier = pltpu.get_barrier_semaphore()

    @pl.when(early)
    def _():
        for k in range(n - 1, FIRST_LATE - 1, -1):
            pl.semaphore_signal(barrier, inc=1, device_id={"date": k}, device_id_type=MESH)

        @pl.loop(0, FIRST_LATE)
        def _(k):
            @pl.when(k != me)
            def _():
                pl.semaphore_signal(barrier, inc=1, device_id={"date": k}, device_id_type=MESH)

    for copy in small:
        copy.start()
    for c in range(5):
        load(c).start()

    for copy in small[:4]:
        copy.wait()
    taps = [[[table[frac[d, x] * 8 + j] for j in range(8)] for x in range(2)] for d in range(2)]
    a_hi, a_lo = split(azimuth_matrix((saz[0], saz[1]), (taps[0][0], taps[1][0])))
    a_both = jnp.concatenate([a_hi, a_lo], axis=0)
    b_both = []
    for d in range(2):
        b_hi, b_lo = split(range_matrix(srg[d], taps[d][1]))
        b_both.append(jnp.concatenate([b_hi, b_lo], axis=1))

    def resample(c):
        load(c).wait()
        y = dot(a_both, slab[:, piece(c)])
        hi, lo = split(y[:64] + y[64:])
        for d in range(2):
            along[d, :32, piece(c)] = hi[32 * d : 32 * d + 32]
            along[d, 32:, piece(c)] = lo[32 * d : 32 * d + 32]
        first, many = FIRST[c], FIRST[c + 1] - FIRST[c]
        for d in range(2):
            whole = along[d, :, pl.ds(first * BLOCK, (many + 1) * BLOCK)]
            rows = jnp.concatenate([whole[:, BLOCK * b : BLOCK * b + 256] for b in range(many)], axis=0)
            y = dot(rows, b_both[d]).reshape(many, 64, 256)
            full = y[:, :32, :128] + (y[:, :32, 128:] + y[:, 32:, :128])
            tx[pl.ds(first, many), pl.ds(32 * d, 32)] = full.astype(BF16)

    def class_of(k):
        return ((k + n - FIRST_LATE) // n) * (k // 4 - PLANES + 1)

    def block_copy(src, dst):
        return pltpu.make_async_remote_copy(
            src_ref=tx.at[dst], dst_ref=rx.at[src],
            send_sem=send_sem.at[class_of(dst)], recv_sem=recv_sem.at[class_of(src)],
            device_id={"date": dst}, device_id_type=MESH,
        )

    def wait_class(c, full, mine, received):
        for count, here in ((full - 1, mine), (full, jnp.logical_not(mine))):

            @pl.when(here)
            def _():
                copy = pltpu.make_async_remote_copy(
                    src_ref=tx.at[pl.ds(0, count)], dst_ref=rx.at[pl.ds(0, count)],
                    send_sem=send_sem.at[c], recv_sem=recv_sem.at[c],
                    device_id={"date": (me + 1) % n}, device_id_type=MESH,
                )
                copy.wait_recv() if received else copy.wait_send()

    def send(lo, hi):
        @pl.loop(lo, hi)
        def _(k):
            @pl.when(k != me)
            def _():
                block_copy(me, k).start()

    late = jnp.logical_not(early)

    @pl.when(early)
    def _():
        pl.semaphore_wait(barrier, FIRST_LATE - 1)

    @pl.when(late)
    def _():
        pl.semaphore_wait(barrier, FIRST_LATE)
        for k in range(FIRST_LATE):
            pl.semaphore_signal(late_sem.at[plane - PLANES], inc=1, device_id={"date": k}, device_id_type=MESH)

    resample(0)
    send(0, 4)
    resample(1)
    send(4, 8)
    resample(2)
    send(8, FIRST_LATE)
    resample(3)
    resample(4)
    rx[me] = tx[me]

    small[4].wait()
    row, col = iota((32, 32), 0), iota((32, 32), 1)
    want = ((row // 4) % 2) * 16 + (row % 4) * 4 + row // 8
    order = jnp.where(col == want, 1.0, 0.0).astype(BF16)
    p = dot(order, prim[...]).reshape(4, 8, 128)
    swapped = jnp.concatenate([p[:, 4:], p[:, :4]], axis=1)

    look = (iota((256, 128), 0) % 128) // 16
    box = jnp.where(look == (iota((256, 128), 1) % 32) // 4, 1.0, 0.0).astype(BF16)
    sub, lane = iota((8, 128), 0), iota((8, 128), 1)
    hit = jnp.where(sub % 4 == lane % 4, 1.0 / 64.0, 0.0)
    part = lane // 32
    masks = (
        jnp.where(part == 0, hit, 0.0),
        jnp.where(part == 1, jnp.where(sub < 4, -hit, hit), 0.0),
        jnp.where(part >= 2, hit, 0.0),
    )

    def boxes(x):
        hi, lo = split(x)
        return dot(jnp.concatenate([hi, lo], axis=1), box)

    power = jnp.sum(boxes(jnp.sum(p * p, axis=0)) * hit, axis=0, keepdims=True)

    row, col = iota((64, 256), 0), iota((64, 256), 1)
    gap = (row - col % 64).astype(F32)
    w = jnp.exp(-(gap * gap) / 128.0)
    total = jnp.sum(jnp.where(col < 64, w, 0.0), axis=1, keepdims=True)
    high = jnp.where(gap == 0.0, 1.0, 0.0) - w / total
    h_hi, h_lo = split(high)
    filt = jnp.where((col // 64) % 2 == 0, h_hi.astype(F32), h_lo.astype(F32)).astype(BF16)

    @pl.when(late)
    def _():
        pl.semaphore_wait(go_sem, 1)
        send(FIRST_LATE, n)

    def held(to):
        return ((plane == 1) & (to >= 6)) | ((plane == 2) & (to >= 6)) | ((plane == 3) & (to >= 7))

    @pl.when(early)
    def _():
        @pl.loop(PLANES, 8)
        def _(to):
            pl.semaphore_wait(late_sem.at[to - PLANES], 4)

            @pl.when(jnp.logical_not(held(to)))
            def _():
                send(4 * to, 4 * to + 4)

    @pl.when(plane == 0)
    def _():
        for to in (6, 7):
            pl.semaphore_signal(go_sem, inc=1, device_id={"date": me % 4 + 4 * to}, device_id_type=MESH)

    @pl.when(plane == 3)
    def _():
        for to in (4, 5):
            pl.semaphore_signal(go_sem, inc=1, device_id={"date": me % 4 + 4 * to}, device_id_type=MESH)

    def turn():
        @pl.when(plane == 0)
        def _():
            wait_class(2, 4, plane == 5, False)

            @pl.loop(1, PLANES)
            def _(k):
                pl.semaphore_signal(turn_sem, inc=1, device_id={"date": me + 4 * k}, device_id_type=MESH)

        @pl.when(early & (plane > 0))
        def _():
            pl.semaphore_wait(turn_sem, 1)

            @pl.loop(PLANES, 8)
            def _(to):
                @pl.when(held(to))
                def _():
                    send(4 * to, 4 * to + 4)

    def process(rows):
        count = 2 * rows.shape[0]
        s = rows.astype(F32).reshape(count, 4, 8, 128)
        kinds = [jnp.sum(s * p[None], axis=1), jnp.sum(s * swapped[None], axis=1), jnp.sum(s * s, axis=1)]
        y = boxes(jnp.stack(kinds, axis=1).reshape(count * 24, 128)).reshape(count, 3, 8, 128)
        z = y[:, 0] * masks[0][None] + y[:, 1] * masks[1][None] + y[:, 2] * masks[2][None]
        return jnp.sum(z, axis=1)

    wait_class(0, FIRST_LATE, early, False)
    wait_class(0, FIRST_LATE, early, True)
    z_ref[pl.ds(0, 2 * FIRST_LATE)] = process(rx[:FIRST_LATE])
    turn()
    wait_class(1, 4, plane == 4, True)
    wait_class(2, 4, plane == 5, True)
    z_ref[pl.ds(32, 16)] = process(rx[16:24])
    wait_class(3, 4, plane == 6, True)
    wait_class(4, 4, plane == 7, True)
    z_ref[pl.ds(48, 16)] = process(rx[24:32])

    z = z_ref[...]
    q = jnp.where(iota((64, 128), 1) < 64, pltpu.roll(z, 64, 1), 1.0)
    c = z * (8.0 / jnp.sqrt((power + 1e-06) * (q + 1e-06)))
    c_hi, c_lo = split(c)
    out = dot(filt, jnp.concatenate([c_hi, c_hi, c_lo, c_lo], axis=0)).T
    out_ref[0] = out[:32]
    out_ref[1] = out[32:64]

    for to in range(PLANES, 8):
        if to != 5:
            wait_class(to - PLANES + 1, 4, plane == to, False)

    @pl.when(plane != 0)
    def _():
        wait_class(2, 4, plane == 5, False)


def shards(primary, secondaries, shift_az, shift_rg, frac_index):
    n = NB
    hbm = pl.BlockSpec(memory_space=pl.ANY)
    operands = (
        shift_az, shift_rg, frac_index, jnp.asarray(tap_table()), primary.reshape(32, 128), secondaries.reshape(128, WIDTH),
    )
    operands = [pltpu.with_memory_space_constraint(x, pltpu.HBM) for x in operands]
    out = pl.pallas_call(
        kernel,
        out_shape=pltpu.VMEM((2, 32, 64), F32),
        in_specs=[hbm] * 6,
        out_specs=pl.BlockSpec(memory_space=pltpu.VMEM),
        scratch_shapes=[
            pltpu.SMEM((2,), jnp.int32),
            pltpu.SMEM((2,), jnp.int32),
            pltpu.SMEM((2, 2), jnp.int32),
            pltpu.SMEM((512,), F32),
            pltpu.VMEM((32, 128), BF16),
            pltpu.VMEM((128, WIDTH), BF16),
            pltpu.VMEM((2, 64, WIDTH), BF16),
            pltpu.VMEM((n, 64, 128), BF16),
            pltpu.VMEM((n, 64, 128), BF16),
            pltpu.VMEM((64, 128), F32),
            pltpu.SemaphoreType.DMA((10,)),
            pltpu.SemaphoreType.DMA((9 - PLANES,)),
            pltpu.SemaphoreType.DMA((9 - PLANES,)),
            pltpu.SemaphoreType.REGULAR((8 - PLANES,)),
            pltpu.SemaphoreType.REGULAR,
            pltpu.SemaphoreType.REGULAR,
        ],
        compiler_params=pltpu.CompilerParams(
            collective_id=0, has_side_effects=True, vmem_limit_bytes=48 * 2**20
        ),
    )(*operands)
    return jnp.transpose(out, (0, 2, 1))


def solution(mesh):
    in_specs = (
        P("tile", None, "date"),
        P("date", "tile", None, None),
        P(("tile", "date")),
        P(("tile", "date")),
        P("date", "tile"),
    )
    out_specs = P("tile", None, "date")
    return jax.shard_map(shards, mesh=mesh, in_specs=in_specs, out_specs=out_specs, check_vma=False)
```

```python
import jax
import jax.numpy as jnp
import numpy as np
from jax import lax
from jax.experimental import pallas as pl
from jax.experimental.pallas import tpu as pltpu
from jax.sharding import PartitionSpec as P

F32 = jnp.float32
BF16 = jnp.bfloat16
WIDTH = 4224
BLOCK = 128
NB = 32
PLANES = 4
FIRST_LATE = 4 * PLANES
PIECES = (0, 5, 9, 17, 25, 33)
FIRST = (0, 4, 8, 16, 24, 32)
MESH = pl.DeviceIdType.MESH


def iota(shape, dim):
    return lax.broadcasted_iota(jnp.int32, shape, dim)


def split(x):
    hi = x.astype(BF16)
    return hi, (x - hi.astype(F32)).astype(BF16)


def dot(a, b):
    return jnp.dot(a, b, preferred_element_type=F32)


def tap_table():
    t = np.arange(8)[None] - 3.0 - np.arange(64)[:, None] / 64.0
    return (np.sinc(t) * (0.5 + 0.5 * np.cos(np.pi * t / 4.0))).astype(np.float32).reshape(-1)


def azimuth_matrix(a, taps):
    row, col = iota((32, 128), 0), iota((32, 128), 1)
    line = (row % 4) * 4 + row // 8
    same = (row // 4) % 2 == (col // 32) % 2
    dates = []
    for d in range(2):
        u = col % 32 - line - a[d]
        u = jnp.where(same & (col // 64 == d), u, -1)
        out = jnp.zeros((32, 128), F32)
        for j in range(8):
            out = jnp.where(u == j, taps[d][j], out)
        dates.append(out)
    return jnp.concatenate(dates, axis=0)


def range_matrix(r, taps):
    u = (iota((8, 128), 0) - iota((8, 128), 1) - r + 256) % 128
    rows = jnp.zeros((8, 128), F32)
    for j in range(8):
        rows = jnp.where(u == j, taps[j], rows)
    turned = [rows] + [pltpu.roll(rows, 8 * k, 1) for k in range(1, 16)]
    u = iota((256, 128), 0) - iota((256, 128), 1) - r
    return jnp.where((u >= 0) & (u < 8), jnp.concatenate(turned * 2, axis=0), 0.0)


def kernel(
    saz_ref, srg_ref, frac_ref, table_ref, prim_ref, sec_ref, out_ref,
    saz, srg, frac, table, prim, slab, along, tx, rx, z_ref, in_sem, send_sem, recv_sem, late_sem, go_sem, turn_sem,
):
    n = NB
    me = lax.axis_index("date")
    plane = me // 4
    early = me < FIRST_LATE

    small = [
        pltpu.make_async_copy(src, dst, in_sem.at[k])
        for k, (src, dst) in enumerate(((saz_ref, saz), (srg_ref, srg), (frac_ref, frac), (table_ref, table), (prim_ref, prim)))
    ]

    def piece(c):
        return pl.ds(PIECES[c] * BLOCK, (PIECES[c + 1] - PIECES[c]) * BLOCK)

    def load(c):
        return pltpu.make_async_copy(sec_ref.at[:, piece(c)], slab.at[:, piece(c)], in_sem.at[5 + c])

    barrier = pltpu.get_barrier_semaphore()

    @pl.when(early)
    def _():
        for k in range(n - 1, FIRST_LATE - 1, -1):
            pl.semaphore_signal(barrier, inc=1, device_id={"date": k}, device_id_type=MESH)

        @pl.loop(0, FIRST_LATE)
        def _(k):
            @pl.when(k != me)
            def _():
                pl.semaphore_signal(barrier, inc=1, device_id={"date": k}, device_id_type=MESH)

    for copy in small:
        copy.start()
    for c in range(5):
        load(c).start()

    for copy in small[:4]:
        copy.wait()
    taps = [[[table[frac[d, x] * 8 + j] for j in range(8)] for x in range(2)] for d in range(2)]
    a_hi, a_lo = split(azimuth_matrix((saz[0], saz[1]), (taps[0][0], taps[1][0])))
    a_both = jnp.concatenate([a_hi, a_lo], axis=0)
    b_both = []
    for d in range(2):
        b_hi, b_lo = split(range_matrix(srg[d], taps[d][1]))
        b_both.append(jnp.concatenate([b_hi, b_lo], axis=1))

    def resample(c):
        load(c).wait()
        y = dot(a_both, slab[:, piece(c)])
        hi, lo = split(y[:64] + y[64:])
        for d in range(2):
            along[d, :32, piece(c)] = hi[32 * d : 32 * d + 32]
            along[d, 32:, piece(c)] = lo[32 * d : 32 * d + 32]
        first, many = FIRST[c], FIRST[c + 1] - FIRST[c]
        for d in range(2):
            whole = along[d, :, pl.ds(first * BLOCK, (many + 1) * BLOCK)]
            rows = jnp.concatenate([whole[:, BLOCK * b : BLOCK * b + 256] for b in range(many)], axis=0)
            y = dot(rows, b_both[d]).reshape(many, 64, 256)
            full = y[:, :32, :128] + (y[:, :32, 128:] + y[:, 32:, :128])
            tx[pl.ds(first, many), pl.ds(32 * d, 32)] = full.astype(BF16)

    def class_of(k):
        return ((k + n - FIRST_LATE) // n) * (k // 4 - PLANES + 1)

    def block_copy(src, dst):
        return pltpu.make_async_remote_copy(
            src_ref=tx.at[dst], dst_ref=rx.at[src],
            send_sem=send_sem.at[class_of(dst)], recv_sem=recv_sem.at[class_of(src)],
            device_id={"date": dst}, device_id_type=MESH,
        )

    def wait_class(c, full, mine, received):
        for count, here in ((full - 1, mine), (full, jnp.logical_not(mine))):

            @pl.when(here)
            def _():
                copy = pltpu.make_async_remote_copy(
                    src_ref=tx.at[pl.ds(0, count)], dst_ref=rx.at[pl.ds(0, count)],
                    send_sem=send_sem.at[c], recv_sem=recv_sem.at[c],
                    device_id={"date": (me + 1) % n}, device_id_type=MESH,
                )
                copy.wait_recv() if received else copy.wait_send()

    def send(lo, hi):
        @pl.loop(lo, hi)
        def _(k):
            @pl.when(k != me)
            def _():
                block_copy(me, k).start()

    late = jnp.logical_not(early)

    @pl.when(early)
    def _():
        pl.semaphore_wait(barrier, FIRST_LATE - 1)

    @pl.when(late)
    def _():
        pl.semaphore_wait(barrier, FIRST_LATE)
        for k in range(FIRST_LATE):
            pl.semaphore_signal(late_sem.at[plane - PLANES], inc=1, device_id={"date": k}, device_id_type=MESH)

    resample(0)
    send(0, 4)
    resample(1)
    send(4, 8)
    resample(2)
    send(8, FIRST_LATE)
    resample(3)
    resample(4)
    rx[me] = tx[me]

    small[4].wait()
    row, col = iota((32, 32), 0), iota((32, 32), 1)
    want = ((row // 4) % 2) * 16 + (row % 4) * 4 + row // 8
    order = jnp.where(col == want, 1.0, 0.0).astype(BF16)
    p = dot(order, prim[...]).reshape(4, 8, 128)
    swapped = jnp.concatenate([p[:, 4:], p[:, :4]], axis=1)

    look = (iota((256, 128), 0) % 128) // 16
    box = jnp.where(look == (iota((256, 128), 1) % 32) // 4, 1.0, 0.0).astype(BF16)
    sub, lane = iota((8, 128), 0), iota((8, 128), 1)
    hit = jnp.where(sub % 4 == lane % 4, 1.0 / 64.0, 0.0)
    part = lane // 32
    masks = (
        jnp.where(part == 0, hit, 0.0),
        jnp.where(part == 1, jnp.where(sub < 4, -hit, hit), 0.0),
        jnp.where(part >= 2, hit, 0.0),
    )

    def boxes(x):
        hi, lo = split(x)
        return dot(jnp.concatenate([hi, lo], axis=1), box)

    power = jnp.sum(boxes(jnp.sum(p * p, axis=0)) * hit, axis=0, keepdims=True)

    row, col = iota((64, 256), 0), iota((64, 256), 1)
    gap = (row - col % 64).astype(F32)
    w = jnp.exp(-(gap * gap) / 128.0)
    total = jnp.sum(jnp.where(col < 64, w, 0.0), axis=1, keepdims=True)
    high = jnp.where(gap == 0.0, 1.0, 0.0) - w / total
    h_hi, h_lo = split(high)
    filt = jnp.where((col // 64) % 2 == 0, h_hi.astype(F32), h_lo.astype(F32)).astype(BF16)

    @pl.when(late)
    def _():
        pl.semaphore_wait(go_sem, 1)
        send(FIRST_LATE, n)

    def held(to):
        return ((plane > 0) & (to >= 7)) | ((plane == 1) & (to >= 6))

    @pl.when(early)
    def _():
        @pl.loop(PLANES, 8)
        def _(to):
            pl.semaphore_wait(late_sem.at[to - PLANES], 4)

            @pl.when(jnp.logical_not(held(to)))
            def _():
                send(4 * to, 4 * to + 4)

    @pl.when(plane == 0)
    def _():
        for to in (6, 7):
            pl.semaphore_signal(go_sem, inc=1, device_id={"date": me % 4 + 4 * to}, device_id_type=MESH)

    @pl.when(plane == 3)
    def _():
        for to in (4, 5):
            pl.semaphore_signal(go_sem, inc=1, device_id={"date": me % 4 + 4 * to}, device_id_type=MESH)

    def turn():
        @pl.when(plane == 0)
        def _():
            wait_class(2, 4, plane == 5, False)

            @pl.loop(1, PLANES)
            def _(k):
                pl.semaphore_signal(turn_sem, inc=1, device_id={"date": me + 4 * k}, device_id_type=MESH)

        @pl.when(early & (plane > 0))
        def _():
            pl.semaphore_wait(turn_sem, 1)

            @pl.loop(PLANES, 8)
            def _(to):
                @pl.when(held(to))
                def _():
                    send(4 * to, 4 * to + 4)

    def process(rows):
        count = 2 * rows.shape[0]
        s = rows.astype(F32).reshape(count, 4, 8, 128)
        kinds = [jnp.sum(s * p[None], axis=1), jnp.sum(s * swapped[None], axis=1), jnp.sum(s * s, axis=1)]
        y = boxes(jnp.stack(kinds, axis=1).reshape(count * 24, 128)).reshape(count, 3, 8, 128)
        z = y[:, 0] * masks[0][None] + y[:, 1] * masks[1][None] + y[:, 2] * masks[2][None]
        return jnp.sum(z, axis=1)

    wait_class(0, FIRST_LATE, early, False)
    wait_class(0, FIRST_LATE, early, True)
    z_ref[pl.ds(0, 2 * FIRST_LATE)] = process(rx[:FIRST_LATE])
    turn()
    wait_class(1, 4, plane == 4, True)
    wait_class(2, 4, plane == 5, True)
    z_ref[pl.ds(32, 16)] = process(rx[16:24])
    wait_class(3, 4, plane == 6, True)
    wait_class(4, 4, plane == 7, True)
    z_ref[pl.ds(48, 16)] = process(rx[24:32])

    z = z_ref[...]
    q = jnp.where(iota((64, 128), 1) < 64, pltpu.roll(z, 64, 1), 1.0)
    c = z * (8.0 / jnp.sqrt((power + 1e-06) * (q + 1e-06)))
    c_hi, c_lo = split(c)
    out = dot(filt, jnp.concatenate([c_hi, c_hi, c_lo, c_lo], axis=0)).T
    out_ref[0] = out[:32]
    out_ref[1] = out[32:64]

    for to in range(PLANES, 8):
        if to != 5:
            wait_class(to - PLANES + 1, 4, plane == to, False)

    @pl.when(plane != 0)
    def _():
        wait_class(2, 4, plane == 5, False)


def shards(primary, secondaries, shift_az, shift_rg, frac_index):
    n = NB
    hbm = pl.BlockSpec(memory_space=pl.ANY)
    operands = (
        shift_az, shift_rg, frac_index, jnp.asarray(tap_table()), primary.reshape(32, 128), secondaries.reshape(128, WIDTH),
    )
    operands = [pltpu.with_memory_space_constraint(x, pltpu.HBM) for x in operands]
    out = pl.pallas_call(
        kernel,
        out_shape=pltpu.VMEM((2, 32, 64), F32),
        in_specs=[hbm] * 6,
        out_specs=pl.BlockSpec(memory_space=pltpu.VMEM),
        scratch_shapes=[
            pltpu.SMEM((2,), jnp.int32),
            pltpu.SMEM((2,), jnp.int32),
            pltpu.SMEM((2, 2), jnp.int32),
            pltpu.SMEM((512,), F32),
            pltpu.VMEM((32, 128), BF16),
            pltpu.VMEM((128, WIDTH), BF16),
            pltpu.VMEM((2, 64, WIDTH), BF16),
            pltpu.VMEM((n, 64, 128), BF16),
            pltpu.VMEM((n, 64, 128), BF16),
            pltpu.VMEM((64, 128), F32),
            pltpu.SemaphoreType.DMA((10,)),
            pltpu.SemaphoreType.DMA((9 - PLANES,)),
            pltpu.SemaphoreType.DMA((9 - PLANES,)),
            pltpu.SemaphoreType.REGULAR((8 - PLANES,)),
            pltpu.SemaphoreType.REGULAR,
            pltpu.SemaphoreType.REGULAR,
        ],
        compiler_params=pltpu.CompilerParams(
            collective_id=0, has_side_effects=True, vmem_limit_bytes=48 * 2**20
        ),
    )(*operands)
    return jnp.transpose(out, (0, 2, 1))


def solution(mesh):
    in_specs = (
        P("tile", None, "date"),
        P("date", "tile", None, None),
        P(("tile", "date")),
        P(("tile", "date")),
        P("date", "tile"),
    )
    out_specs = P("tile", None, "date")
    return jax.shard_map(shards, mesh=mesh, in_specs=in_specs, out_specs=out_specs, check_vma=False)
```

```python
import jax
import jax.numpy as jnp
import numpy as np
from jax import lax
from jax.experimental import pallas as pl
from jax.experimental.pallas import tpu as pltpu
from jax.sharding import PartitionSpec as P

F32 = jnp.float32
BF16 = jnp.bfloat16
WIDTH = 4224
BLOCK = 128
NB = 32
PLANES = 4
FIRST_LATE = 4 * PLANES
PIECES = (0, 5, 9, 17, 25, 33)
FIRST = (0, 4, 8, 16, 24, 32)
MESH = pl.DeviceIdType.MESH


def iota(shape, dim):
    return lax.broadcasted_iota(jnp.int32, shape, dim)


def split(x):
    hi = x.astype(BF16)
    return hi, (x - hi.astype(F32)).astype(BF16)


def dot(a, b):
    return jnp.dot(a, b, preferred_element_type=F32)


def tap_table():
    t = np.arange(8)[None] - 3.0 - np.arange(64)[:, None] / 64.0
    return (np.sinc(t) * (0.5 + 0.5 * np.cos(np.pi * t / 4.0))).astype(np.float32).reshape(-1)


def azimuth_matrix(a, taps):
    row, col = iota((32, 128), 0), iota((32, 128), 1)
    line = (row % 4) * 4 + row // 8
    same = (row // 4) % 2 == (col // 32) % 2
    dates = []
    for d in range(2):
        u = col % 32 - line - a[d]
        u = jnp.where(same & (col // 64 == d), u, -1)
        out = jnp.zeros((32, 128), F32)
        for j in range(8):
            out = jnp.where(u == j, taps[d][j], out)
        dates.append(out)
    return jnp.concatenate(dates, axis=0)


def range_matrix(r, taps):
    u = (iota((8, 128), 0) - iota((8, 128), 1) - r + 256) % 128
    rows = jnp.zeros((8, 128), F32)
    for j in range(8):
        rows = jnp.where(u == j, taps[j], rows)
    turned = [rows] + [pltpu.roll(rows, 8 * k, 1) for k in range(1, 16)]
    u = iota((256, 128), 0) - iota((256, 128), 1) - r
    return jnp.where((u >= 0) & (u < 8), jnp.concatenate(turned * 2, axis=0), 0.0)


def kernel(
    saz_ref, srg_ref, frac_ref, table_ref, prim_ref, sec_ref, out_ref,
    saz, srg, frac, table, prim, slab, along, tx, rx, z_ref, in_sem, send_sem, recv_sem, late_sem, go_sem, turn_sem,
):
    n = NB
    me = lax.axis_index("date")
    plane = me // 4
    early = me < FIRST_LATE

    small = [
        pltpu.make_async_copy(src, dst, in_sem.at[k])
        for k, (src, dst) in enumerate(((saz_ref, saz), (srg_ref, srg), (frac_ref, frac), (table_ref, table), (prim_ref, prim)))
    ]

    def piece(c):
        return pl.ds(PIECES[c] * BLOCK, (PIECES[c + 1] - PIECES[c]) * BLOCK)

    def load(c):
        return pltpu.make_async_copy(sec_ref.at[:, piece(c)], slab.at[:, piece(c)], in_sem.at[5 + c])

    barrier = pltpu.get_barrier_semaphore()

    @pl.when(early)
    def _():
        for k in range(n - 1, FIRST_LATE - 1, -1):
            pl.semaphore_signal(barrier, inc=1, device_id={"date": k}, device_id_type=MESH)

        @pl.loop(0, FIRST_LATE)
        def _(k):
            @pl.when(k != me)
            def _():
                pl.semaphore_signal(barrier, inc=1, device_id={"date": k}, device_id_type=MESH)

    for copy in small:
        copy.start()
    for c in range(5):
        load(c).start()

    for copy in small[:4]:
        copy.wait()
    taps = [[[table[frac[d, x] * 8 + j] for j in range(8)] for x in range(2)] for d in range(2)]
    a_hi, a_lo = split(azimuth_matrix((saz[0], saz[1]), (taps[0][0], taps[1][0])))
    a_both = jnp.concatenate([a_hi, a_lo], axis=0)
    b_both = []
    for d in range(2):
        b_hi, b_lo = split(range_matrix(srg[d], taps[d][1]))
        b_both.append(jnp.concatenate([b_hi, b_lo], axis=1))

    def resample(c):
        load(c).wait()
        y = dot(a_both, slab[:, piece(c)])
        hi, lo = split(y[:64] + y[64:])
        for d in range(2):
            along[d, :32, piece(c)] = hi[32 * d : 32 * d + 32]
            along[d, 32:, piece(c)] = lo[32 * d : 32 * d + 32]
        first, many = FIRST[c], FIRST[c + 1] - FIRST[c]
        for d in range(2):
            whole = along[d, :, pl.ds(first * BLOCK, (many + 1) * BLOCK)]
            rows = jnp.concatenate([whole[:, BLOCK * b : BLOCK * b + 256] for b in range(many)], axis=0)
            y = dot(rows, b_both[d]).reshape(many, 64, 256)
            full = y[:, :32, :128] + (y[:, :32, 128:] + y[:, 32:, :128])
            tx[pl.ds(first, many), pl.ds(32 * d, 32)] = full.astype(BF16)

    def class_of(k):
        return ((k + n - FIRST_LATE) // n) * (k // 4 - PLANES + 1)

    def block_copy(src, dst):
        return pltpu.make_async_remote_copy(
            src_ref=tx.at[dst], dst_ref=rx.at[src],
            send_sem=send_sem.at[class_of(dst)], recv_sem=recv_sem.at[class_of(src)],
            device_id={"date": dst}, device_id_type=MESH,
        )

    def wait_class(c, full, mine, received):
        for count, here in ((full - 1, mine), (full, jnp.logical_not(mine))):

            @pl.when(here)
            def _():
                copy = pltpu.make_async_remote_copy(
                    src_ref=tx.at[pl.ds(0, count)], dst_ref=rx.at[pl.ds(0, count)],
                    send_sem=send_sem.at[c], recv_sem=recv_sem.at[c],
                    device_id={"date": (me + 1) % n}, device_id_type=MESH,
                )
                copy.wait_recv() if received else copy.wait_send()

    def send(lo, hi):
        @pl.loop(lo, hi)
        def _(k):
            @pl.when(k != me)
            def _():
                block_copy(me, k).start()

    late = jnp.logical_not(early)

    @pl.when(early)
    def _():
        pl.semaphore_wait(barrier, FIRST_LATE - 1)

    @pl.when(late)
    def _():
        pl.semaphore_wait(barrier, FIRST_LATE)
        for k in range(FIRST_LATE):
            pl.semaphore_signal(late_sem.at[plane - PLANES], inc=1, device_id={"date": k}, device_id_type=MESH)

    resample(0)
    send(0, 4)
    resample(1)
    send(4, 8)
    resample(2)
    send(8, FIRST_LATE)
    resample(3)
    resample(4)
    rx[me] = tx[me]

    small[4].wait()
    row, col = iota((32, 32), 0), iota((32, 32), 1)
    want = ((row // 4) % 2) * 16 + (row % 4) * 4 + row // 8
    order = jnp.where(col == want, 1.0, 0.0).astype(BF16)
    p = dot(order, prim[...]).reshape(4, 8, 128)
    swapped = jnp.concatenate([p[:, 4:], p[:, :4]], axis=1)

    look = (iota((256, 128), 0) % 128) // 16
    box = jnp.where(look == (iota((256, 128), 1) % 32) // 4, 1.0, 0.0).astype(BF16)
    sub, lane = iota((8, 128), 0), iota((8, 128), 1)
    hit = jnp.where(sub % 4 == lane % 4, 1.0 / 64.0, 0.0)
    part = lane // 32
    masks = (
        jnp.where(part == 0, hit, 0.0),
        jnp.where(part == 1, jnp.where(sub < 4, -hit, hit), 0.0),
        jnp.where(part >= 2, hit, 0.0),
    )

    def boxes(x):
        hi, lo = split(x)
        return dot(jnp.concatenate([hi, lo], axis=1), box)

    power = jnp.sum(boxes(jnp.sum(p * p, axis=0)) * hit, axis=0, keepdims=True)

    row, col = iota((64, 256), 0), iota((64, 256), 1)
    gap = (row - col % 64).astype(F32)
    w = jnp.exp(-(gap * gap) / 128.0)
    total = jnp.sum(jnp.where(col < 64, w, 0.0), axis=1, keepdims=True)
    high = jnp.where(gap == 0.0, 1.0, 0.0) - w / total
    h_hi, h_lo = split(high)
    filt = jnp.where((col // 64) % 2 == 0, h_hi.astype(F32), h_lo.astype(F32)).astype(BF16)

    @pl.when(late)
    def _():
        pl.semaphore_wait(go_sem, 1)
        send(FIRST_LATE, n)

    def held(to):
        return ((plane == 1) & (to >= 6)) | ((plane == 2) & (to >= 6)) | ((plane == 3) & (to >= 7))

    @pl.when(early)
    def _():
        @pl.loop(PLANES, 8)
        def _(to):
            pl.semaphore_wait(late_sem.at[to - PLANES], 4)

            @pl.when(jnp.logical_not(held(to)))
            def _():
                send(4 * to, 4 * to + 4)

    @pl.when(plane == 0)
    def _():
        for to in (6, 7):
            pl.semaphore_signal(go_sem, inc=1, device_id={"date": me % 4 + 4 * to}, device_id_type=MESH)

    @pl.when(plane == 3)
    def _():
        for to in (4, 5):
            pl.semaphore_signal(go_sem, inc=1, device_id={"date": me % 4 + 4 * to}, device_id_type=MESH)

    def turn():
        @pl.when(plane == 0)
        def _():
            wait_class(2, 4, plane == 5, False)

            @pl.loop(1, PLANES)
            def _(k):
                pl.semaphore_signal(turn_sem, inc=1, device_id={"date": me + 4 * k}, device_id_type=MESH)

        @pl.when(early & (plane > 0))
        def _():
            pl.semaphore_wait(turn_sem, 1)

            @pl.loop(PLANES, 8)
            def _(to):
                @pl.when(held(to))
                def _():
                    send(4 * to, 4 * to + 4)

    def process(rows):
        count = 2 * rows.shape[0]
        s = rows.astype(F32).reshape(count, 4, 8, 128)
        kinds = [jnp.sum(s * p[None], axis=1), jnp.sum(s * swapped[None], axis=1), jnp.sum(s * s, axis=1)]
        y = boxes(jnp.stack(kinds, axis=1).reshape(count * 24, 128)).reshape(count, 3, 8, 128)
        z = y[:, 0] * masks[0][None] + y[:, 1] * masks[1][None] + y[:, 2] * masks[2][None]
        return jnp.sum(z, axis=1)

    wait_class(0, FIRST_LATE, early, False)
    wait_class(0, FIRST_LATE, early, True)
    z_ref[pl.ds(0, 2 * FIRST_LATE)] = process(rx[:FIRST_LATE])
    turn()
    wait_class(1, 4, plane == 4, True)
    wait_class(2, 4, plane == 5, True)
    z_ref[pl.ds(32, 16)] = process(rx[16:24])
    wait_class(3, 4, plane == 6, True)
    z_ref[pl.ds(48, 8)] = process(rx[24:28])
    wait_class(4, 4, plane == 7, True)
    z_ref[pl.ds(56, 8)] = process(rx[28:32])

    z = z_ref[...]
    q = jnp.where(iota((64, 128), 1) < 64, pltpu.roll(z, 64, 1), 1.0)
    c = z * (8.0 / jnp.sqrt((power + 1e-06) * (q + 1e-06)))
    c_hi, c_lo = split(c)
    out = dot(filt, jnp.concatenate([c_hi, c_hi, c_lo, c_lo], axis=0)).T
    out_ref[0] = out[:32]
    out_ref[1] = out[32:64]

    for to in range(PLANES, 8):
        if to != 5:
            wait_class(to - PLANES + 1, 4, plane == to, False)

    @pl.when(plane != 0)
    def _():
        wait_class(2, 4, plane == 5, False)


def shards(primary, secondaries, shift_az, shift_rg, frac_index):
    n = NB
    hbm = pl.BlockSpec(memory_space=pl.ANY)
    operands = (
        shift_az, shift_rg, frac_index, jnp.asarray(tap_table()), primary.reshape(32, 128), secondaries.reshape(128, WIDTH),
    )
    operands = [pltpu.with_memory_space_constraint(x, pltpu.HBM) for x in operands]
    out = pl.pallas_call(
        kernel,
        out_shape=pltpu.VMEM((2, 32, 64), F32),
        in_specs=[hbm] * 6,
        out_specs=pl.BlockSpec(memory_space=pltpu.VMEM),
        scratch_shapes=[
            pltpu.SMEM((2,), jnp.int32),
            pltpu.SMEM((2,), jnp.int32),
            pltpu.SMEM((2, 2), jnp.int32),
            pltpu.SMEM((512,), F32),
            pltpu.VMEM((32, 128), BF16),
            pltpu.VMEM((128, WIDTH), BF16),
            pltpu.VMEM((2, 64, WIDTH), BF16),
            pltpu.VMEM((n, 64, 128), BF16),
            pltpu.VMEM((n, 64, 128), BF16),
            pltpu.VMEM((64, 128), F32),
            pltpu.SemaphoreType.DMA((10,)),
            pltpu.SemaphoreType.DMA((9 - PLANES,)),
            pltpu.SemaphoreType.DMA((9 - PLANES,)),
            pltpu.SemaphoreType.REGULAR((8 - PLANES,)),
            pltpu.SemaphoreType.REGULAR,
            pltpu.SemaphoreType.REGULAR,
        ],
        compiler_params=pltpu.CompilerParams(
            collective_id=0, has_side_effects=True, vmem_limit_bytes=48 * 2**20
        ),
    )(*operands)
    return jnp.transpose(out, (0, 2, 1))


def solution(mesh):
    in_specs = (
        P("tile", None, "date"),
        P("date", "tile", None, None),
        P(("tile", "date")),
        P(("tile", "date")),
        P("date", "tile"),
    )
    out_specs = P("tile", None, "date")
    return jax.shard_map(shards, mesh=mesh, in_specs=in_specs, out_specs=out_specs, check_vma=False)
```
